128 devices in a mesh: cube: 128 (over x, y, z, core).
Axes of the slice: x: 4, y: 4, z: 4, core: 2. Of those that a mesh axis runs over, the one named last changes fastest.
Arguments:
- vectors: bfloat16 [524288, 768], P('cube'), may hold values from -40 to 40
- child_labels: int32 [2, 524288], P(None, 'cube'), may hold values from 0 to 1, as said below
Outputs:
- held: bfloat16 [917504, 768], P('cube')
- margin_one: float32 [786432], P('cube')
- margin_two: float32 [917504], P('cube')
- centroids: float32 [6, 768], replicated
The draws below stay inside these ranges and needn't reach their ends.
Inputs may be any that keep to these rules, and one draw needn't show every extreme that they name: `child_labels`: per device, the vectors leaving at the first level number from 1024 to 2048, and 2048 on some device in every draw. `child_labels`: per device, the second-level leavers among its vectors that stay at the first level number at most 512, and among the vectors it sends away at the first level at most 512; in every draw some device holds 512 second-level leavers of each kind (its own stayers and those received at the first level), so its second-level send buffer is full.
All inputs are finite; a program needn't handle non-finite values.
Results may differ from the reference program's by a relative error of at most 0.0011.
Values may be sent and summed in bfloat16 or wider, within the bound.
A program may use at most 128 MiB of HBM per device.

```python
from functools import partial
import jax
import jax.numpy as jnp

D = 768
ROWS = 4096
N_CUBE = 128


def label_plan(key):
    ways = N_CUBE
    levels = ways.bit_length() - 1
    cap_one = ROWS // 2
    cap_two = ROWS // 4
    device = jnp.arange(ways, dtype=jnp.int32)
    bit_one = device >> levels - 1 & 1
    bit_two = device >> levels - 2 & 1
    keys = jax.random.split(key, 5)
    orders = jax.vmap(lambda k: jax.random.permutation(k, ROWS))(jax.random.split(keys[0], ways))
    rank = jnp.argsort(orders, axis=1).astype(jnp.int32)
    hot = jax.random.randint(keys[1], (), 0, ways)
    sends = jax.random.randint(keys[2], (ways,), cap_one // 2, cap_one + 1)
    sends = jnp.where(device == hot, cap_one, sends)
    stays_out = jax.random.randint(keys[3], (ways,), cap_two // 4, cap_two // 2 + 1)
    stays_out = jnp.where(device == hot, cap_two // 2, stays_out)
    sent_out = jax.random.randint(keys[4], (ways,), cap_two // 4, cap_two // 2 + 1)
    sent_out = jnp.where(device == hot ^ 1 << levels - 1, cap_two // 2, sent_out)
    miss_one = rank < sends[:, None]
    miss_two = jnp.where(miss_one, rank < sent_out[:, None], rank - sends[:, None] < stays_out[:, None])
    first = bit_one[:, None] ^ miss_one.astype(jnp.int32)
    later = bit_two[:, None] ^ miss_two.astype(jnp.int32)
    return (first.reshape(-1), later.reshape(-1))


def draw_child_labels(key, part):
    first, later = label_plan(key)
    return jnp.stack([first, later]).astype(jnp.int32)


def draw_vectors(key, part):
    first, later = label_plan(key)
    key = jax.random.fold_in(key, 7)
    keys = jax.random.split(key, 3)
    ways = N_CUBE
    device = jnp.arange(ways * ROWS) // ROWS
    spread = 3.0 ** (device.astype(jnp.float32) / (ways - 1))
    axis_one = jax.random.normal(keys[0], (D,), jnp.float32)
    axis_two = jax.random.normal(keys[1], (D,), jnp.float32)
    noise = jax.random.normal(keys[2], (ways * ROWS, D), jnp.float32)
    sign_one = (2 * first - 1).astype(jnp.float32)[:, None]
    sign_two = (2 * later - 1).astype(jnp.float32)[:, None]
    signal = 0.6 * spread[:, None] * (sign_one * axis_one[None] + sign_two * axis_two[None])
    return jnp.clip(noise + signal, -40.0, 40.0).astype(jnp.bfloat16)


def setup_inputs(seed: int = 0) -> dict:
    seeds = jax.random.split(jax.random.key(seed), 3)
    vectors = draw_vectors(jax.random.fold_in(seeds[2], 71), 0)
    child_labels = draw_child_labels(jax.random.fold_in(seeds[2], 71), 0)
    return dict(vectors=vectors, child_labels=child_labels)


def compact(mask, rows, cap, fill):
    place = jnp.cumsum(mask.astype(jnp.int32)) - 1
    index = jnp.where(mask, place, cap).astype(jnp.int32)
    base = jnp.full((cap + 1,) + rows.shape[1:], fill, rows.dtype)
    return base.at[index].set(rows)[:cap]


def split_margin(held_rows, live, pair):
    scores = jnp.dot(held_rows, pair.astype(jnp.bfloat16).T, preferred_element_type=jnp.float32)
    offset = 0.5 * (jnp.sum(pair[1] * pair[1]) - jnp.sum(pair[0] * pair[0]))
    return jnp.where(live, (scores[:, 1] - scores[:, 0] - offset) / D, jnp.float32(0.0))


def group_sum(values, group, count):
    return jnp.stack([jnp.sum(jnp.where((group == g)[:, None], values, jnp.float32(0.0)), axis=0) for g in range(count)])


def reference(vectors, child_labels):
    ways = N_CUBE
    levels = ways.bit_length() - 1
    device = jnp.arange(ways, dtype=jnp.int32)
    bit_one = (device >> (levels - 1)) & 1
    bit_two = (device >> (levels - 2)) & 1
    rows = vectors.reshape(ways, ROWS, D)
    first = child_labels[0].reshape(ways, ROWS)
    later = child_labels[1].reshape(ways, ROWS)
    cap_one = ROWS // 2
    cap_two = ROWS // 4
    leave = first != bit_one[:, None]
    stay = jnp.logical_not(leave)
    send_rows = jax.vmap(partial(compact, cap=cap_one, fill=0))(leave, rows)
    send_tags = jax.vmap(partial(compact, cap=cap_one, fill=-1))(leave, later)
    partner = device ^ (1 << (levels - 1))
    held_one = jnp.concatenate([jnp.where(stay[..., None], rows, jnp.zeros((), jnp.bfloat16)), send_rows[partner]], axis=1)
    tags = jnp.concatenate([jnp.where(stay, later, -1), send_tags[partner]], axis=1)
    live_one = tags >= 0
    sum_one = jnp.sum(held_one, axis=1, dtype=jnp.float32)
    count_one = jnp.sum(live_one, axis=1).astype(jnp.float32)
    centre_one = group_sum(sum_one, bit_one, 2) / group_sum(count_one[:, None], bit_one, 2)
    margin_one = jax.vmap(split_margin, in_axes=(0, 0, None))(held_one, live_one, centre_one)
    moving = live_one & (tags != bit_two[:, None])
    out_rows = jax.vmap(partial(compact, cap=cap_two, fill=0))(moving, held_one)
    out_tags = jax.vmap(partial(compact, cap=cap_two, fill=-1))(moving, tags)
    other = device ^ (1 << (levels - 2))
    held_two = jnp.concatenate([jnp.where(moving[..., None], jnp.zeros((), jnp.bfloat16), held_one), out_rows[other]], axis=1)
    live_two = jnp.concatenate([live_one & jnp.logical_not(moving), out_tags[other] >= 0], axis=1)
    group = 2 * bit_one + bit_two
    sum_two = jnp.sum(held_two, axis=1, dtype=jnp.float32)
    count_two = jnp.sum(live_two, axis=1).astype(jnp.float32)
    centre_two = group_sum(sum_two, group, 4) / group_sum(count_two[:, None], group, 4)
    pairs = centre_two.reshape(2, 2, D)[bit_one]
    margin_two = jax.vmap(split_margin)(held_two, live_two, pairs)
    centroids = jnp.concatenate([centre_one, centre_two], axis=0)
    return (held_two.reshape(ways * (ROWS + cap_one + cap_two), D), margin_one.reshape(-1), margin_two.reshape(-1), centroids)
```

```python
import jax
import jax.numpy as jnp
from jax import lax
from jax.experimental import pallas as pl
from jax.experimental.pallas import tpu as pltpu
from jax.sharding import PartitionSpec as P

MESH = pl.DeviceIdType.MESH
ROWS = 4096
WIDTH = 768
CAP_ONE = 2048
CAP_TWO = 1024
HALF = 512
CHUNK = 256
HELD = ROWS + CAP_ONE + CAP_TWO
F32 = jnp.float32
BF16 = jnp.bfloat16

CHUNKS = 12


def split3(v):
    hi = v.astype(BF16).astype(F32)
    mid = (v - hi).astype(BF16).astype(F32)
    lo = v - hi - mid
    return hi, mid, lo


def stack_rows(rows, count):
    at = lax.broadcasted_iota(jnp.int32, (count, rows[0].shape[1]), 0)
    out = jnp.zeros(at.shape, rows[0].dtype)
    for k, row in enumerate(rows):
        out = jnp.where(at == k, row, out)
    return out


def exchange_kernel(
    x_ref, lab_ref,
    held, m1, m2, cent,
    xv, ybuf, dland, lhs, rk, acc, accs, arl, vmat, ms_c, ms_b, ms_d, ml_c, ml_b, ml_d,
    load_sem, ar_send, ar_recv, row_send, row_recv, m_send, m_recv,
):
    me = lax.axis_index("cube")
    xi = me // 32
    yi = (me // 8) % 4
    zi = (me // 2) % 4
    t = me // 64
    u = xi % 2

    def three(i, stride):
        return [
            me + stride * (1 - 2 * (i % 2)),
            me + stride * (2 - 4 * (i // 2)),
            me + stride * (3 - 2 * i),
        ]

    x1, x2, x3 = three(xi, 32)
    phases = [[x1, x2, x3], three(zi, 2), three(yi, 8), [me + 1 - 2 * (me % 2)]]
    partners = [d for phase in phases for d in phase]

    barrier = pltpu.get_barrier_semaphore()
    for d in partners:
        pl.semaphore_signal(barrier, inc=1, device_id=(d,), device_id_type=MESH)

    loads = [
        pltpu.make_async_copy(x_ref.at[pl.ds(i * 1024, 1024)], xv.at[pl.ds(i * 1024, 1024)], load_sem.at[i])
        for i in range(4)
    ]
    for c in loads:
        c.start()

    first = lab_ref[0:1, :]
    later = lab_ref[1:2, :]
    leave = first != t
    move = later != u
    f_leave = jnp.where(leave, 1.0, 0.0)
    f_move = jnp.where(move, 1.0, 0.0)
    f_b = f_move * (1.0 - f_leave)
    f_d = f_move * f_leave
    kinds = stack_rows([f_leave, f_b, f_d], 16).astype(BF16)
    tri = jnp.where(
        lax.broadcasted_iota(jnp.int32, (256, 256), 0) <= lax.broadcasted_iota(jnp.int32, (256, 256), 1), 1.0, 0.0
    ).astype(BF16)
    carry = jnp.full((16, 1), -1.0, F32)
    for k in range(ROWS // 256):
        part = kinds[:, 256 * k : 256 * k + 256]
        run = jnp.dot(part, tri, preferred_element_type=F32) + carry
        carry = run[:, 255:256]
        place = run.astype(jnp.int32)
        s = pl.ds(256 * k, 256)
        lv = leave[:, 256 * k : 256 * k + 256]
        mv = move[:, 256 * k : 256 * k + 256]
        none = jnp.full((1, 256), -1, jnp.int32)
        rk[0:1, s] = jnp.where(mv, none, jnp.where(lv, place[0:1], none))
        rk[1:2, s] = jnp.where(lv, none, jnp.where(mv, place[1:2], none))
        rk[2:3, s] = jnp.where(lv, jnp.where(mv, place[2:3], none), none)
        rk[3:4, s] = jnp.where(lv, place[0:1], none)
    n_b = carry[1:2, 0:1] + 1.0

    def one_hot(row, base):
        for k in range(ROWS // 256):
            s = pl.ds(256 * k, 256)
            at = lax.broadcasted_iota(jnp.int32, (CHUNK, 256), 0)
            want = rk[pl.ds(row, 1), s] - base
            lhs[0:CHUNK, s] = jnp.where(at == want, 1.0, 0.0).astype(BF16)

    one_hot(0, 0)
    group = 2 * first + later
    masks = stack_rows([jnp.where(group == g, 1.0, 0.0) for g in range(4)], 16)
    lhs[CHUNK : CHUNK + 16, :] = masks.astype(BF16)
    count = jnp.sum(masks[0:4], axis=1, keepdims=True)
    for c in loads:
        c.wait()
    out = jnp.dot(lhs[...], xv[...], preferred_element_type=F32)
    ybuf[0:CHUNK, :] = out[0:CHUNK].astype(BF16)
    accs[0, 0:4, :] = out[CHUNK : CHUNK + 4]
    accs[0, 4:8, :] = jnp.broadcast_to(count, (4, WIDTH))
    pl.semaphore_wait(barrier, len(partners))

    def ar_copies(p):
        base = 3 * p
        return [
            pltpu.make_async_remote_copy(
                src_ref=accs.at[p], dst_ref=arl.at[base + i], send_sem=ar_send.at[base + i],
                recv_sem=ar_recv.at[base + i], device_id=(d,), device_id_type=MESH,
            )
            for i, d in enumerate(phases[p])
        ]

    def ar_start(p):
        for c in ar_copies(p):
            c.start()

    def ar_finish(p):
        for c in ar_copies(p):
            c.wait()
        if p < 3:
            total = (accs[p] + arl[3 * p]) + (arl[3 * p + 1] + arl[3 * p + 2])
            accs[p + 1] = total
        else:
            acc[...] = accs[3] + arl[9]

    def c_copy(q):
        j = jnp.where(q == 0, 0, q - 4)
        return pltpu.make_async_remote_copy(
            src_ref=ybuf.at[pl.ds(pl.multiple_of(q * CHUNK, CHUNK), CHUNK)],
            dst_ref=held.at[pl.ds(pl.multiple_of(ROWS + j * CHUNK, CHUNK), CHUNK)],
            send_sem=row_send.at[q], recv_sem=row_recv.at[q], device_id=(x2,), device_id_type=MESH,
        )

    def b_copy(q):
        return pltpu.make_async_remote_copy(
            src_ref=ybuf.at[pl.ds(pl.multiple_of(q * CHUNK, CHUNK), CHUNK)],
            dst_ref=held.at[pl.ds(pl.multiple_of(ROWS + CAP_ONE + (q - 1) * CHUNK, CHUNK), CHUNK)],
            send_sem=row_send.at[q], recv_sem=row_recv.at[q], device_id=(x1,), device_id_type=MESH,
        )

    def d_copy(q):
        return pltpu.make_async_remote_copy(
            src_ref=ybuf.at[pl.ds(pl.multiple_of(q * CHUNK, CHUNK), CHUNK)],
            dst_ref=dland.at[pl.ds(pl.multiple_of((q - 3) * CHUNK, CHUNK), CHUNK)],
            send_sem=row_send.at[q], recv_sem=row_recv.at[q], device_id=(x3,), device_id_type=MESH,
        )

    ar_start(0)
    c_copy(0).start()

    def compact(q, row, base):
        one_hot(row, base)
        res = jnp.dot(lhs[0:CHUNK, :], xv[...], preferred_element_type=F32)
        ybuf[pl.ds(pl.multiple_of(q * CHUNK, CHUNK), CHUNK), :] = res.astype(BF16)

    def early(q, _):
        row = jnp.where(q < 3, 1, jnp.where(q < 5, 2, 0))
        base = CHUNK * jnp.where(q < 3, q - 1, jnp.where(q < 5, q - 3, q - 4))
        compact(q, row, base)

        @pl.when(q < 3)
        def _():
            b_copy(q).start()

        @pl.when((q >= 3) & (q < 5))
        def _():
            d_copy(q).start()

        @pl.when(q >= 5)
        def _():
            c_copy(q).start()

        for p in range(4):
            @pl.when(q == p + 1)
            def _(p=p):
                ar_finish(p)
                if p < 3:
                    ar_start(p + 1)

        return 0

    lax.fori_loop(1, 9, early, 0)

    tot = acc[...]
    c2 = tot[0:4] / tot[4:8]
    pair_sum = jnp.concatenate([tot[0:1] + tot[1:2], tot[2:3] + tot[3:4]], axis=0)
    pair_num = jnp.concatenate([tot[4:5] + tot[5:6], tot[6:7] + tot[7:8]], axis=0)
    c1 = pair_sum / pair_num
    cent[0:2, :] = c1
    cent[2:6, :] = c2
    six = jnp.concatenate([c1, c2, jnp.zeros((2, WIDTH), F32)], axis=0)
    norm = jnp.sum(six * six, axis=1, keepdims=True)
    off_one = 0.5 * (norm[1:2] - norm[0:1])
    off_low = 0.5 * (norm[3:4] - norm[2:3])
    off_high = 0.5 * (norm[5:6] - norm[4:5])
    sixb = jnp.concatenate([six, jnp.zeros((8, WIDTH), F32)], axis=0).astype(BF16)

    def margins(k, _):
        s = pl.ds(pl.multiple_of(k * 512, 512), 512)
        sc = lax.dot_general(sixb, xv[s, :], (((1,), (1,)), ((), ())), preferred_element_type=F32)
        fk = lab_ref[0:1, s]
        mk = lab_ref[1:2, s] != u
        lk = fk != t
        one = (sc[1:2] - sc[0:1] - off_one) / WIDTH
        two = jnp.where(fk == 1, sc[5:6] - sc[4:5] - off_high, sc[3:4] - sc[2:3] - off_low) / WIDTH
        m1[0:1, s] = jnp.where(lk, 0.0, one)
        m2[0:1, s] = jnp.where(lk, 0.0, jnp.where(mk, 0.0, two))
        two_c = jnp.where(mk, 0.0, two)
        vmat[:, s] = stack_rows([*split3(one), *split3(two_c), *split3(two)], 16).astype(BF16)
        return 0

    lax.fori_loop(0, 8, margins, 0)

    def pack_margins(row, base):
        one_hot(row, base)
        return lax.dot_general(
            vmat[...], lhs[0:CHUNK, :], (((1,), (1,)), ((), ())), preferred_element_type=F32
        )

    def pack_c(j, _):
        r = pack_margins(3, CHUNK * j)
        s = pl.ds(pl.multiple_of(j * CHUNK, CHUNK), CHUNK)
        ms_c[0:1, s] = r[0:1] + r[1:2] + r[2:3]
        ms_c[1:2, s] = r[3:4] + r[4:5] + r[5:6]
        return 0

    def pack_bd(j, _):
        r = pack_margins(1 + j // 2, CHUNK * (j % 2))
        s = pl.ds(pl.multiple_of((j % 2) * CHUNK, CHUNK), CHUNK)
        v = r[6:7] + r[7:8] + r[8:9]

        @pl.when(j < 2)
        def _():
            ms_b[0:1, s] = v

        @pl.when(j >= 2)
        def _():
            ms_d[0:1, s] = v

        return 0

    ms_b[1:2, :] = jnp.broadcast_to(n_b, (1, HALF))
    ms_d[1:2, :] = jnp.zeros((1, HALF), F32)
    lax.fori_loop(0, 4, pack_bd, 0)
    m_copies = [
        pltpu.make_async_remote_copy(
            src_ref=src, dst_ref=dst, send_sem=m_send.at[i], recv_sem=m_recv.at[i], device_id=(d,), device_id_type=MESH,
        )
        for i, (src, dst, d) in enumerate([(ms_b, ml_b, x1), (ms_d, ml_d, x3), (ms_c, ml_c, x2)])
    ]
    m_copies[0].start()
    m_copies[1].start()
    lax.fori_loop(0, 8, pack_c, 0)
    m_copies[2].start()

    def late(q, _):
        compact(q, 0, CHUNK * (q - 4))
        c_copy(q).start()
        return 0

    lax.fori_loop(9, CHUNKS, late, 0)

    def keep(k, _):
        s = pl.ds(pl.multiple_of(k * 256, 256), 256)
        stay = jnp.where(lab_ref[0:1, s] == t, jnp.where(lab_ref[1:2, s] == u, 1.0, 0.0), 0.0)
        eye = lax.broadcasted_iota(jnp.int32, (256, 256), 0) == lax.broadcasted_iota(jnp.int32, (256, 256), 1)
        pick = jnp.where(eye, stay, 0.0).astype(BF16)
        held[s, :] = jnp.dot(pick, xv[s, :], preferred_element_type=F32).astype(BF16)
        return 0

    lax.fori_loop(0, ROWS // 256, keep, 0)

    for c in m_copies[:2]:
        c.wait()
    for q in (1, 2):
        b_copy(q).wait()
    for q in (3, 4):
        d_copy(q).wait()
    shift = ml_b[1:2, 0:1].astype(jnp.int32)

    def place(k, _):
        base = k * 256
        s = pl.ds(pl.multiple_of(ROWS + CAP_ONE + base, 256), 256)
        slot = lax.broadcasted_iota(jnp.int32, (256, HALF), 0) + base
        src = lax.broadcasted_iota(jnp.int32, (256, HALF), 1) + shift
        hot = jnp.where(slot == src, 1.0, 0.0).astype(BF16)
        rows = jnp.dot(hot, dland[...], preferred_element_type=F32)

        @pl.when(k < 2)
        def _():
            held[s, :] = (rows + held[s, :].astype(F32)).astype(BF16)

        @pl.when(k >= 2)
        def _():
            held[s, :] = rows.astype(BF16)

        return 0

    lax.fori_loop(0, 4, place, 0)
    dm = stack_rows(list(split3(ml_d[0:1, :])), 16).astype(BF16)
    src = lax.broadcasted_iota(jnp.int32, (HALF, CAP_TWO), 0) + shift
    slot = lax.broadcasted_iota(jnp.int32, (HALF, CAP_TWO), 1)
    moved = jnp.dot(dm, jnp.where(slot == src, 1.0, 0.0).astype(BF16), preferred_element_type=F32)
    moved = moved[0:1] + moved[1:2] + moved[2:3]
    m2[0:1, ROWS + CAP_ONE : ROWS + CAP_ONE + HALF] = moved[:, 0:HALF] + ml_b[0:1, :]
    m2[0:1, ROWS + CAP_ONE + HALF : HELD] = moved[:, HALF:CAP_TWO]
    m_copies[2].wait()
    m1[0:1, ROWS : ROWS + CAP_ONE] = ml_c[0:1, :]
    m2[0:1, ROWS : ROWS + CAP_ONE] = ml_c[1:2, :]

    for q in (0, 5, 6, 7, 8, 9, 10, 11):
        c_copy(q).wait()


PIECES = 14


def store_kernel(held, m1, m2, cent, held_out, m1_out, m2_out, cent_out, sem):
    step = HELD // PIECES
    copies = [
        pltpu.make_async_copy(held.at[pl.ds(i * step, step)], held_out.at[pl.ds(i * step, step)], sem.at[i])
        for i in range(PIECES)
    ]
    for i, (src, dst) in enumerate([(m1, m1_out), (m2, m2_out), (cent, cent_out)]):
        copies.append(pltpu.make_async_copy(src, dst, sem.at[PIECES + i]))
    for c in copies:
        c.start()
    for c in copies:
        c.wait()


def local(vectors, child_labels):
    in_vmem = pl.BlockSpec(memory_space=pltpu.VMEM)
    anywhere = pl.BlockSpec(memory_space=pl.ANY)
    shapes = [((HELD, WIDTH), BF16), ((1, ROWS + CAP_ONE), F32), ((1, HELD), F32), ((6, WIDTH), F32)]
    dma = pltpu.SemaphoreType.DMA
    parts = pl.pallas_call(
        exchange_kernel,
        out_shape=tuple(pltpu.VMEM(s, d) for s, d in shapes),
        in_specs=[anywhere, in_vmem],
        out_specs=(in_vmem,) * 4,
        scratch_shapes=[
            pltpu.VMEM((ROWS, WIDTH), BF16),
            pltpu.VMEM((CHUNKS * CHUNK, WIDTH), BF16),
            pltpu.VMEM((HALF, WIDTH), BF16),
            pltpu.VMEM((CHUNK + 16, ROWS), BF16),
            pltpu.VMEM((8, ROWS), jnp.int32),
            pltpu.VMEM((8, WIDTH), F32),
            pltpu.VMEM((4, 8, WIDTH), F32),
            pltpu.VMEM((10, 8, WIDTH), F32),
            pltpu.VMEM((16, ROWS), BF16),
            pltpu.VMEM((2, CAP_ONE), F32),
            pltpu.VMEM((2, HALF), F32),
            pltpu.VMEM((2, HALF), F32),
            pltpu.VMEM((2, CAP_ONE), F32),
            pltpu.VMEM((2, HALF), F32),
            pltpu.VMEM((2, HALF), F32),
            dma((4,)),
            dma((10,)),
            dma((10,)),
            dma((CHUNKS,)),
            dma((CHUNKS,)),
            dma((3,)),
            dma((3,)),
        ],
        compiler_params=pltpu.CompilerParams(
            collective_id=0, has_side_effects=True, vmem_limit_bytes=44 << 20
        ),
        name="exchange",
    )(vectors, child_labels)
    held, m1, m2, cent = pl.pallas_call(
        store_kernel,
        out_shape=tuple(jax.ShapeDtypeStruct(s, d) for s, d in shapes),
        in_specs=[in_vmem] * 4,
        out_specs=(anywhere,) * 4,
        scratch_shapes=[dma((PIECES + 3,))],
        compiler_params=pltpu.CompilerParams(vmem_limit_bytes=16 << 20),
        name="store",
    )(*parts)
    return held, m1.reshape(-1), m2.reshape(-1), cent


def solution(mesh):
    return jax.shard_map(
        local,
        mesh=mesh,
        in_specs=(P("cube", None), P(None, "cube")),
        out_specs=(P("cube", None), P("cube"), P("cube"), P()),
        check_vma=False,
    )
```

```python
import jax
import jax.numpy as jnp
from jax import lax
from jax.experimental import pallas as pl
from jax.experimental.pallas import tpu as pltpu
from jax.sharding import PartitionSpec as P

MESH = pl.DeviceIdType.MESH
ROWS = 4096
WIDTH = 768
CAP_ONE = 2048
CAP_TWO = 1024
HALF = 512
LOAD = 1024
AHEAD = 2
PIECE = 512
CHUNK = 256
HELD = ROWS + CAP_ONE + CAP_TWO
F32 = jnp.float32
BF16 = jnp.bfloat16

HEAD = 128
MID = 4
C_CHUNKS = 8
B_AT = HEAD + C_CHUNKS * CHUNK
D_AT = B_AT + HALF
PACKED = D_AT + HALF
SUM_ROWS = 16


def split3(v):
    hi = v.astype(BF16).astype(F32)
    mid = (v - hi).astype(BF16).astype(F32)
    lo = v - hi - mid
    return hi, mid, lo


def stack_rows(rows, count):
    at = lax.broadcasted_iota(jnp.int32, (count, rows[0].shape[1]), 0)
    out = jnp.zeros(at.shape, rows[0].dtype)
    for k, row in enumerate(rows):
        out = jnp.where(at == k, row, out)
    return out


def exchange_kernel(
    x_ref, lab_any,
    held, m1, m2, cent,
    xv, lab_ref, ybuf, dland, lhs, rk, acc, accs, arl, vmat, ms_c, ms_b, ms_d, ml_c, ml_b, ml_d,
    load_sem, ar_send, ar_recv, row_send, row_recv, m_send, m_recv,
):
    me = lax.axis_index("cube")
    loads = [
        pltpu.make_async_copy(x_ref.at[pl.ds(i * LOAD, LOAD)], xv.at[pl.ds(i * LOAD, LOAD)], load_sem.at[i])
        for i in range(ROWS // LOAD)
    ]
    lab_load = pltpu.make_async_copy(lab_any, lab_ref, load_sem.at[ROWS // LOAD])
    lab_load.start()
    for c in loads[:AHEAD]:
        c.start()
    xi = me // 32
    yi = (me // 8) % 4
    zi = (me // 2) % 4
    t = me // 64
    u = xi % 2

    def three(i, stride):
        return [
            me + stride * (1 - 2 * (i % 2)),
            me + stride * (2 - 4 * (i // 2)),
            me + stride * (3 - 2 * i),
        ]

    x1, x2, x3 = three(xi, 32)
    z1, z2, _ = three(zi, 2)
    y1, y2, _ = three(yi, 8)
    phases = [[x1, x2, x3], [z1], [z2], [y1], [y2], [me + 1 - 2 * (me % 2)]]
    slots = [0, 3, 4, 5, 6, 7]
    partners = [d for phase in phases for d in phase]

    barrier = pltpu.get_barrier_semaphore()
    for d in partners:
        pl.semaphore_signal(barrier, inc=1, device_id=(d,), device_id_type=MESH)

    lab_load.wait()

    first = lab_ref[0:1, :]
    later = lab_ref[1:2, :]
    leave = first != t
    move = later != u
    f_leave = jnp.where(leave, 1.0, 0.0)
    f_move = jnp.where(move, 1.0, 0.0)
    f_b = f_move * (1.0 - f_leave)
    f_d = f_move * f_leave
    kinds = stack_rows([f_leave, f_b, f_d], 16)
    tri = jnp.where(
        lax.broadcasted_iota(jnp.int32, (256, 256), 0) <= lax.broadcasted_iota(jnp.int32, (256, 256), 1), 1.0, 0.0
    ).astype(BF16)
    carry = jnp.full((16, 1), -1.0, F32)
    for k in range(ROWS // 256):
        part = kinds[:, 256 * k : 256 * k + 256]
        run = jnp.dot(part.astype(BF16), tri, preferred_element_type=F32) + carry
        carry = carry + jnp.sum(part, axis=1, keepdims=True)
        place = run.astype(jnp.int32)
        s = pl.ds(256 * k, 256)
        lv = leave[:, 256 * k : 256 * k + 256]
        mv = move[:, 256 * k : 256 * k + 256]
        none = jnp.full((1, 256), -1, jnp.int32)
        rk[0:1, s] = jnp.where(mv, none, jnp.where(lv, place[0:1], none))
        rk[1:2, s] = jnp.where(lv, none, jnp.where(mv, place[1:2], none))
        rk[2:3, s] = jnp.where(lv, jnp.where(mv, place[2:3], none), none)
        rk[3:4, s] = jnp.where(lv, place[0:1], none)
    n_b = carry[1:2, 0:1] + 1.0

    def one_hot(row, base):
        for k in range(ROWS // 256):
            s = pl.ds(256 * k, 256)
            at = lax.broadcasted_iota(jnp.int32, (CHUNK, 256), 0)
            want = rk[pl.ds(row, 1), s] - base
            lhs[0:CHUNK, s] = jnp.where(at == want, 1.0, 0.0).astype(BF16)

    def hot_piece(row, base, count, at, size):
        slot = lax.broadcasted_iota(jnp.int32, (count, size), 0)
        return jnp.where(slot == rk[pl.ds(row, 1), pl.ds(at, size)] - base, 1.0, 0.0).astype(BF16)

    out = jnp.zeros((HEAD, WIDTH), F32)
    for i, c in enumerate(loads):
        c.wait()
        if i + AHEAD < len(loads):
            loads[i + AHEAD].start()
        hot = hot_piece(0, 0, HEAD, i * LOAD, LOAD)
        out = out + jnp.dot(hot, xv[pl.ds(i * LOAD, LOAD), :], preferred_element_type=F32)
    ybuf[0:HEAD, :] = out.astype(BF16)
    pl.semaphore_wait(barrier, len(partners))

    LAST = len(phases) - 1

    def ar_copies(p):
        base = slots[p]
        return [
            pltpu.make_async_remote_copy(
                src_ref=accs.at[p], dst_ref=arl.at[base + i], send_sem=ar_send.at[base + i],
                recv_sem=ar_recv.at[base + i], device_id=(d,), device_id_type=MESH,
            )
            for i, d in enumerate(phases[p])
        ]

    def ar_start(p):
        for c in ar_copies(p):
            c.start()

    def ar_finish(p):
        for c in ar_copies(p):
            c.wait()
        base = slots[p]
        total = accs[p] + arl[base]
        if len(phases[p]) == 3:
            total = total + (arl[base + 1] + arl[base + 2])
        if p < LAST:
            accs[p + 1] = total
        else:
            acc[...] = total

    def rows_copy(k, src, dst, start, count, to):
        return pltpu.make_async_remote_copy(
            src_ref=ybuf.at[pl.ds(pl.multiple_of(src, HEAD), count)],
            dst_ref=dst.at[pl.ds(pl.multiple_of(start, HEAD), count)],
            send_sem=row_send.at[k], recv_sem=row_recv.at[k], device_id=(to,), device_id_type=MESH,
        )

    def c_copy(j, count=CHUNK):
        src = HEAD + j * CHUNK
        return rows_copy(4 + j, src, held, ROWS + src, count, x2)

    def b_copy(j):
        return rows_copy(2 * j, B_AT + j * CHUNK, held, ROWS + CAP_ONE + j * CHUNK, CHUNK, x1)

    def d_copy(j):
        return rows_copy(2 * j + 1, D_AT + j * CHUNK, dland, j * CHUNK, CHUNK, x3)

    head_copy = rows_copy(4 + C_CHUNKS, 0, held, ROWS, HEAD, x2)
    last_copy = c_copy(MID, CAP_ONE - HEAD - MID * CHUNK)
    head_copy.start()

    def compact(row, base, to):
        res = jnp.zeros((CHUNK, WIDTH), F32)
        for k in range(ROWS // PIECE):
            hot = hot_piece(row, base, CHUNK, k * PIECE, PIECE)
            res = res + jnp.dot(hot, xv[pl.ds(k * PIECE, PIECE), :], preferred_element_type=F32)
        ybuf[pl.ds(pl.multiple_of(to, HEAD), CHUNK), :] = res.astype(BF16)

    group = 2 * first + later
    masks = stack_rows([jnp.where(group == g, 1.0, 0.0) for g in range(4)], SUM_ROWS)
    count = jnp.sum(masks[0:4], axis=1, keepdims=True)
    res = jnp.zeros((CHUNK + SUM_ROWS, WIDTH), F32)
    for k in range(ROWS // PIECE):
        hot = hot_piece(0, HEAD, CHUNK, k * PIECE, PIECE)
        both = jnp.concatenate([hot, masks[:, k * PIECE : (k + 1) * PIECE].astype(BF16)], axis=0)
        res = res + jnp.dot(both, xv[pl.ds(k * PIECE, PIECE), :], preferred_element_type=F32)
    ybuf[HEAD : HEAD + CHUNK, :] = res[0:CHUNK].astype(BF16)
    accs[0, :, 0:WIDTH] = res[CHUNK : CHUNK + 4]
    accs[0, :, WIDTH:] = jnp.broadcast_to(count, (4, 128))
    ar_start(0)
    c_copy(0).start()

    def ar_step(p):
        ar_finish(p)
        if p < LAST:
            ar_start(p + 1)

    def early_bd(k, _):
        j = k // 2
        compact(1 + k % 2, CHUNK * j, B_AT + HALF * (k % 2) + CHUNK * j)

        @pl.when(k % 2 == 1)
        def _():
            b_copy(j).start()
            d_copy(j).start()

        for p in range(4):
            @pl.when(k == p)
            def _(p=p):
                ar_step(p)

        return 0

    lax.fori_loop(0, 4, early_bd, 0)

    def early_c(j, _):
        compact(0, HEAD + CHUNK * j, HEAD + CHUNK * j)
        c_copy(j).start()

        for p in range(4, len(phases)):
            @pl.when(j == p - 3)
            def _(p=p):
                ar_step(p)

        return 0

    lax.fori_loop(1, MID, early_c, 0)

    tot = acc[:, 0:WIDTH]
    num = acc[:, WIDTH : WIDTH + 1]
    c2 = tot / num
    pair_sum = jnp.concatenate([tot[0:1] + tot[1:2], tot[2:3] + tot[3:4]], axis=0)
    pair_num = jnp.concatenate([num[0:1] + num[1:2], num[2:3] + num[3:4]], axis=0)
    c1 = pair_sum / pair_num
    cent[0:2, :] = c1
    cent[2:6, :] = c2
    six = jnp.concatenate([c1, c2, jnp.zeros((2, WIDTH), F32)], axis=0)
    norm = jnp.sum(six * six, axis=1, keepdims=True)
    off_one = 0.5 * (norm[1:2] - norm[0:1])
    off_low = 0.5 * (norm[3:4] - norm[2:3])
    off_high = 0.5 * (norm[5:6] - norm[4:5])
    sixb = jnp.concatenate([six, jnp.zeros((8, WIDTH), F32)], axis=0).astype(BF16)

    def margins(k, _):
        s = pl.ds(pl.multiple_of(k * 512, 512), 512)
        sc = lax.dot_general(sixb, xv[s, :], (((1,), (1,)), ((), ())), preferred_element_type=F32)
        fk = lab_ref[0:1, s]
        mk = lab_ref[1:2, s] != u
        lk = fk != t
        one = (sc[1:2] - sc[0:1] - off_one) / WIDTH
        two = jnp.where(fk == 1, sc[5:6] - sc[4:5] - off_high, sc[3:4] - sc[2:3] - off_low) / WIDTH
        m1[0:1, s] = jnp.where(lk, 0.0, one)
        m2[0:1, s] = jnp.where(lk, 0.0, jnp.where(mk, 0.0, two))
        two_c = jnp.where(mk, 0.0, two)
        vmat[:, s] = stack_rows([*split3(one), *split3(two_c), *split3(two)], 16).astype(BF16)
        return 0

    lax.fori_loop(0, 8, margins, 0)

    def pack_margins(row, base):
        one_hot(row, base)
        return lax.dot_general(
            vmat[...], lhs[0:CHUNK, :], (((1,), (1,)), ((), ())), preferred_element_type=F32
        )

    def pack_c(j, _):
        r = pack_margins(3, CHUNK * j)
        s = pl.ds(pl.multiple_of(j * CHUNK, CHUNK), CHUNK)
        ms_c[0:1, s] = r[0:1] + r[1:2] + r[2:3]
        ms_c[1:2, s] = r[3:4] + r[4:5] + r[5:6]
        return 0

    def pack_bd(j, _):
        r = pack_margins(1 + j // 2, CHUNK * (j % 2))
        s = pl.ds(pl.multiple_of((j % 2) * CHUNK, CHUNK), CHUNK)
        v = r[6:7] + r[7:8] + r[8:9]

        @pl.when(j < 2)
        def _():
            ms_b[0:1, s] = v

        @pl.when(j >= 2)
        def _():
            ms_d[0:1, s] = v

        return 0

    ms_b[1:2, :] = jnp.broadcast_to(n_b, (1, HALF))
    ms_d[1:2, :] = jnp.zeros((1, HALF), F32)
    lax.fori_loop(0, 4, pack_bd, 0)
    m_copies = [
        pltpu.make_async_remote_copy(
            src_ref=src, dst_ref=dst, send_sem=m_send.at[i], recv_sem=m_recv.at[i], device_id=(d,), device_id_type=MESH,
        )
        for i, (src, dst, d) in enumerate([(ms_b, ml_b, x1), (ms_d, ml_d, x3), (ms_c, ml_c, x2)])
    ]
    m_copies[0].start()
    m_copies[1].start()
    lax.fori_loop(0, 8, pack_c, 0)
    m_copies[2].start()

    def late(j, _):
        compact(0, HEAD + CHUNK * j, HEAD + CHUNK * j)
        return 0

    lax.fori_loop(MID, C_CHUNKS, late, 0)
    last_copy.start()

    def keep(k, _):
        s = pl.ds(pl.multiple_of(k * 256, 256), 256)
        stay = jnp.where(lab_ref[0:1, s] == t, jnp.where(lab_ref[1:2, s] == u, 1.0, 0.0), 0.0)
        eye = lax.broadcasted_iota(jnp.int32, (256, 256), 0) == lax.broadcasted_iota(jnp.int32, (256, 256), 1)
        pick = jnp.where(eye, stay, 0.0).astype(BF16)
        held[s, :] = jnp.dot(pick, xv[s, :], preferred_element_type=F32).astype(BF16)
        return 0

    lax.fori_loop(0, ROWS // 256, keep, 0)

    for c in m_copies[:2]:
        c.wait()
    for j in range(2):
        b_copy(j).wait()
        d_copy(j).wait()
    shift = ml_b[1:2, 0:1].astype(jnp.int32)

    def place(k, _):
        base = k * 256
        s = pl.ds(pl.multiple_of(ROWS + CAP_ONE + base, 256), 256)
        slot = lax.broadcasted_iota(jnp.int32, (256, HALF), 0) + base
        src = lax.broadcasted_iota(jnp.int32, (256, HALF), 1) + shift
        hot = jnp.where(slot == src, 1.0, 0.0).astype(BF16)
        rows = jnp.dot(hot, dland[...], preferred_element_type=F32)

        @pl.when(k < 2)
        def _():
            held[s, :] = (rows + held[s, :].astype(F32)).astype(BF16)

        @pl.when(k >= 2)
        def _():
            held[s, :] = rows.astype(BF16)

        return 0

    lax.fori_loop(0, 4, place, 0)
    dm = stack_rows(list(split3(ml_d[0:1, :])), 16).astype(BF16)
    src = lax.broadcasted_iota(jnp.int32, (HALF, CAP_TWO), 0) + shift
    slot = lax.broadcasted_iota(jnp.int32, (HALF, CAP_TWO), 1)
    moved = jnp.dot(dm, jnp.where(slot == src, 1.0, 0.0).astype(BF16), preferred_element_type=F32)
    moved = moved[0:1] + moved[1:2] + moved[2:3]
    m2[0:1, ROWS + CAP_ONE : ROWS + CAP_ONE + HALF] = moved[:, 0:HALF] + ml_b[0:1, :]
    m2[0:1, ROWS + CAP_ONE + HALF : HELD] = moved[:, HALF:CAP_TWO]
    m_copies[2].wait()
    m1[0:1, ROWS : ROWS + CAP_ONE] = ml_c[0:1, :]
    m2[0:1, ROWS : ROWS + CAP_ONE] = ml_c[1:2, :]

    head_copy.wait()
    for j in range(MID):
        c_copy(j).wait()
    last_copy.wait()


PIECES = 14


def store_kernel(held, m1, m2, cent, held_out, m1_out, m2_out, cent_out, sem):
    step = HELD // PIECES
    copies = [
        pltpu.make_async_copy(held.at[pl.ds(i * step, step)], held_out.at[pl.ds(i * step, step)], sem.at[i])
        for i in range(PIECES)
    ]
    for i, (src, dst) in enumerate([(m1, m1_out), (m2, m2_out), (cent, cent_out)]):
        copies.append(pltpu.make_async_copy(src, dst, sem.at[PIECES + i]))
    for c in copies:
        c.start()
    for c in copies:
        c.wait()


def local(vectors, child_labels):
    in_vmem = pl.BlockSpec(memory_space=pltpu.VMEM)
    anywhere = pl.BlockSpec(memory_space=pl.ANY)
    shapes = [((HELD, WIDTH), BF16), ((1, ROWS + CAP_ONE), F32), ((1, HELD), F32), ((6, WIDTH), F32)]
    dma = pltpu.SemaphoreType.DMA
    parts = pl.pallas_call(
        exchange_kernel,
        out_shape=tuple(pltpu.VMEM(s, d) for s, d in shapes),
        in_specs=[anywhere, anywhere],
        out_specs=(in_vmem,) * 4,
        scratch_shapes=[
            pltpu.VMEM((ROWS, WIDTH), BF16),
            pltpu.VMEM((2, ROWS), jnp.int32),
            pltpu.VMEM((PACKED, WIDTH), BF16),
            pltpu.VMEM((HALF, WIDTH), BF16),
            pltpu.VMEM((CHUNK, ROWS), BF16),
            pltpu.VMEM((8, ROWS), jnp.int32),
            pltpu.VMEM((4, WIDTH + 128), F32),
            pltpu.VMEM((6, 4, WIDTH + 128), F32),
            pltpu.VMEM((8, 4, WIDTH + 128), F32),
            pltpu.VMEM((16, ROWS), BF16),
            pltpu.VMEM((2, CAP_ONE), F32),
            pltpu.VMEM((2, HALF), F32),
            pltpu.VMEM((2, HALF), F32),
            pltpu.VMEM((2, CAP_ONE), F32),
            pltpu.VMEM((2, HALF), F32),
            pltpu.VMEM((2, HALF), F32),
            dma((ROWS // LOAD + 1,)),
            dma((8,)),
            dma((8,)),
            dma((C_CHUNKS + 5,)),
            dma((C_CHUNKS + 5,)),
            dma((3,)),
            dma((3,)),
        ],
        compiler_params=pltpu.CompilerParams(
            collective_id=0, has_side_effects=True, vmem_limit_bytes=44 << 20
        ),
        name="exchange",
    )(vectors, child_labels)
    held, m1, m2, cent = pl.pallas_call(
        store_kernel,
        out_shape=tuple(jax.ShapeDtypeStruct(s, d) for s, d in shapes),
        in_specs=[in_vmem] * 4,
        out_specs=(anywhere,) * 4,
        scratch_shapes=[dma((PIECES + 3,))],
        compiler_params=pltpu.CompilerParams(vmem_limit_bytes=16 << 20),
        name="store",
    )(*parts)
    return held, m1.reshape(-1), m2.reshape(-1), cent


def solution(mesh):
    return jax.shard_map(
        local,
        mesh=mesh,
        in_specs=(P("cube", None), P(None, "cube")),
        out_specs=(P("cube", None), P("cube"), P("cube"), P()),
        check_vma=False,
    )
```

```python
import jax
import jax.numpy as jnp
from jax import lax
from jax.experimental import pallas as pl
from jax.experimental.pallas import tpu as pltpu
from jax.sharding import PartitionSpec as P

MESH = pl.DeviceIdType.MESH
ROWS = 4096
WIDTH = 768
CAP_ONE = 2048
CAP_TWO = 1024
HALF = 512
LOAD = 1024
AHEAD = 4
PIECE = 512
CHUNK = 256
HELD = ROWS + CAP_ONE + CAP_TWO
F32 = jnp.float32
BF16 = jnp.bfloat16

MOST = 1792
SPLIT = 1536
HEAD = 128
MID = 4
C_CHUNKS = 8
B_AT = HEAD + C_CHUNKS * CHUNK
D_AT = B_AT + HALF
PACKED = D_AT + HALF
SUM_ROWS = 16
LATE = HEAD + MID * CHUNK


def split3(v):
    hi = v.astype(BF16).astype(F32)
    mid = (v - hi).astype(BF16).astype(F32)
    lo = v - hi - mid
    return hi, mid, lo


def stack_rows(rows, count):
    at = lax.broadcasted_iota(jnp.int32, (count, rows[0].shape[1]), 0)
    out = jnp.zeros(at.shape, rows[0].dtype)
    for k, row in enumerate(rows):
        out = jnp.where(at == k, row, out)
    return out


def exchange_kernel(
    x_ref, lab_any,
    held, m1, m2, cent, flag, rest, slots_hbm,
    xv, lab_ref, ybuf, cland, dland, lhs, rk, acc, accs, arl, vmat, ms_c, ms_b, ms_d, ms_s, slots_out, ml_c, ml_b, ml_d,
    load_sem, ar_send, ar_recv, row_send, row_recv, m_send, m_recv,
):
    me = lax.axis_index("cube")
    loads = [
        pltpu.make_async_copy(x_ref.at[pl.ds(i * LOAD, LOAD)], xv.at[pl.ds(i * LOAD, LOAD)], load_sem.at[i])
        for i in range(ROWS // LOAD)
    ]
    lab_load = pltpu.make_async_copy(lab_any, lab_ref, load_sem.at[ROWS // LOAD])
    lab_load.start()
    for c in loads[:AHEAD]:
        c.start()
    xi = me // 32
    yi = (me // 8) % 4
    zi = (me // 2) % 4
    t = me // 64
    u = xi % 2

    def three(i, stride):
        return [
            me + stride * (1 - 2 * (i % 2)),
            me + stride * (2 - 4 * (i // 2)),
            me + stride * (3 - 2 * i),
        ]

    x1, x2, x3 = three(xi, 32)
    z1, z2, _ = three(zi, 2)
    y1, y2, _ = three(yi, 8)
    phases = [[x1, x2, x3], [z1], [z2], [y1], [y2], [me + 1 - 2 * (me % 2)]]
    slots = [0, 3, 4, 5, 6, 7]
    partners = [d for phase in phases for d in phase]

    barrier = pltpu.get_barrier_semaphore()
    for d in partners:
        pl.semaphore_signal(barrier, inc=1, device_id=(d,), device_id_type=MESH)

    lab_load.wait()

    first = lab_ref[0:1, :]
    later = lab_ref[1:2, :]
    leave = first != t
    move = later != u
    f_leave = jnp.where(leave, 1.0, 0.0)
    f_move = jnp.where(move, 1.0, 0.0)
    f_b = f_move * (1.0 - f_leave)
    f_d = f_move * f_leave
    f_c = f_leave * (1.0 - f_move)
    kinds = stack_rows([f_leave, f_b, f_d, f_c], 16)
    tri = jnp.where(
        lax.broadcasted_iota(jnp.int32, (256, 256), 0) <= lax.broadcasted_iota(jnp.int32, (256, 256), 1), 1.0, 0.0
    ).astype(BF16)
    carry = jnp.full((16, 1), -1.0, F32)
    for k in range(ROWS // 256):
        part = kinds[:, 256 * k : 256 * k + 256]
        run = jnp.dot(part.astype(BF16), tri, preferred_element_type=F32) + carry
        carry = carry + jnp.sum(part, axis=1, keepdims=True)
        place = run.astype(jnp.int32)
        s = pl.ds(256 * k, 256)
        lv = leave[:, 256 * k : 256 * k + 256]
        mv = move[:, 256 * k : 256 * k + 256]
        none = jnp.full((1, 256), -1, jnp.int32)
        rk[0:1, s] = jnp.where(mv, none, jnp.where(lv, place[3:4], none))
        rk[1:2, s] = jnp.where(lv, none, jnp.where(mv, place[1:2], none))
        rk[2:3, s] = jnp.where(lv, jnp.where(mv, place[2:3], none), none)
        rk[3:4, s] = jnp.where(lv, place[0:1], none)
    n_b = carry[1:2, 0:1] + 1.0
    n_c = carry[3:4, 0:1] + 1.0

    def one_hot(row, base):
        for k in range(ROWS // 256):
            s = pl.ds(256 * k, 256)
            at = lax.broadcasted_iota(jnp.int32, (CHUNK, 256), 0)
            want = rk[pl.ds(row, 1), s] - base
            lhs[0:CHUNK, s] = jnp.where(at == want, 1.0, 0.0).astype(BF16)

    def hot_piece(row, base, count, at, size):
        slot = lax.broadcasted_iota(jnp.int32, (count, size), 0)
        return jnp.where(slot == rk[pl.ds(row, 1), pl.ds(at, size)] - base, 1.0, 0.0).astype(BF16)

    out = jnp.zeros((HEAD, WIDTH), F32)
    for i, c in enumerate(loads):
        c.wait()
        if i + AHEAD < len(loads):
            loads[i + AHEAD].start()
        hot = hot_piece(0, 0, HEAD, i * LOAD, LOAD)
        out = out + jnp.dot(hot, xv[pl.ds(i * LOAD, LOAD), :], preferred_element_type=F32)
    ybuf[0:HEAD, :] = out.astype(BF16)
    pl.semaphore_wait(barrier, len(partners))

    LAST = len(phases) - 1

    def ar_copies(p):
        base = slots[p]
        return [
            pltpu.make_async_remote_copy(
                src_ref=accs.at[p], dst_ref=arl.at[base + i], send_sem=ar_send.at[base + i],
                recv_sem=ar_recv.at[base + i], device_id=(d,), device_id_type=MESH,
            )
            for i, d in enumerate(phases[p])
        ]

    def ar_start(p):
        for c in ar_copies(p):
            c.start()

    def ar_finish(p):
        for c in ar_copies(p):
            c.wait()
        base = slots[p]
        total = accs[p] + arl[base]
        most = jnp.maximum(accs[p], arl[base])
        if len(phases[p]) == 3:
            total = total + (arl[base + 1] + arl[base + 2])
            most = jnp.maximum(most, jnp.maximum(arl[base + 1], arl[base + 2]))
        is_max = lax.broadcasted_iota(jnp.int32, total.shape, 1) >= WIDTH + 64
        total = jnp.where(is_max, most, total)
        if p < LAST:
            accs[p + 1] = total
        else:
            acc[...] = total

    def rows_copy(k, src, dst, start, count, to):
        return pltpu.make_async_remote_copy(
            src_ref=ybuf.at[pl.ds(pl.multiple_of(src, HEAD), count)],
            dst_ref=dst.at[pl.ds(pl.multiple_of(start, HEAD), count)],
            send_sem=row_send.at[k], recv_sem=row_recv.at[k], device_id=(to,), device_id_type=MESH,
        )

    def c_copy(j, count=CHUNK):
        src = HEAD + j * CHUNK
        return rows_copy(4 + j, src, cland, src, count, x2)

    def b_copy(j):
        return rows_copy(2 * j, B_AT + j * CHUNK, held, ROWS + CAP_ONE + j * CHUNK, CHUNK, x1)

    def d_copy(j):
        return rows_copy(2 * j + 1, D_AT + j * CHUNK, dland, j * CHUNK, CHUNK, x3)

    head_copy = rows_copy(4 + C_CHUNKS, 0, cland, 0, HEAD, x2)
    late_copy = c_copy(MID, SPLIT - LATE)
    last_copy = rows_copy(4 + MID + 1, SPLIT, cland, SPLIT, MOST - SPLIT, x2)
    head_copy.start()

    def compact(row, base, to):
        res = jnp.zeros((CHUNK, WIDTH), F32)
        for k in range(ROWS // PIECE):
            hot = hot_piece(row, base, CHUNK, k * PIECE, PIECE)
            res = res + jnp.dot(hot, xv[pl.ds(k * PIECE, PIECE), :], preferred_element_type=F32)
        ybuf[pl.ds(pl.multiple_of(to, HEAD), CHUNK), :] = res.astype(BF16)

    group = 2 * first + later
    masks = stack_rows([jnp.where(group == g, 1.0, 0.0) for g in range(4)], SUM_ROWS)
    count = jnp.sum(masks[0:4], axis=1, keepdims=True)
    res = jnp.zeros((CHUNK + SUM_ROWS, WIDTH), F32)
    for k in range(ROWS // PIECE):
        hot = hot_piece(0, HEAD, CHUNK, k * PIECE, PIECE)
        both = jnp.concatenate([hot, masks[:, k * PIECE : (k + 1) * PIECE].astype(BF16)], axis=0)
        res = res + jnp.dot(both, xv[pl.ds(k * PIECE, PIECE), :], preferred_element_type=F32)
    ybuf[HEAD : HEAD + CHUNK, :] = res[0:CHUNK].astype(BF16)
    accs[0, :, 0:WIDTH] = res[CHUNK : CHUNK + 4]
    is_max = lax.broadcasted_iota(jnp.int32, (4, WIDTH + 128), 1) >= WIDTH + 64
    accs[0, :, WIDTH:] = jnp.where(is_max[:, WIDTH:], n_c, count)
    ar_start(0)
    c_copy(0).start()

    def ar_step(p):
        ar_finish(p)
        if p < LAST:
            ar_start(p + 1)

    def early_bd(k, _):
        j = k // 2
        compact(1 + k % 2, CHUNK * j, B_AT + HALF * (k % 2) + CHUNK * j)

        @pl.when(k % 2 == 1)
        def _():
            b_copy(j).start()
            d_copy(j).start()

        for p in range(4):
            @pl.when(k == p)
            def _(p=p):
                ar_step(p)

        return 0

    lax.fori_loop(0, 4, early_bd, 0)

    def early_c(j, _):
        compact(0, HEAD + CHUNK * j, HEAD + CHUNK * j)
        c_copy(j).start()

        for p in range(4, len(phases)):
            @pl.when(j == p - 3)
            def _(p=p):
                ar_step(p)

        return 0

    lax.fori_loop(1, MID, early_c, 0)

    def pack_margins(row, base):
        one_hot(row, base)
        return lax.dot_general(
            vmat[...], lhs[0:CHUNK, :], (((1,), (1,)), ((), ())), preferred_element_type=F32
        )

    slot = rk[3:4, :]
    high = slot // 256
    vmat[...] = stack_rows([high.astype(F32), (slot - 256 * high).astype(F32)], 16).astype(BF16)

    def pack_slots(j, _):
        r = pack_margins(0, CHUNK * j)
        s = pl.ds(pl.multiple_of(j * CHUNK, CHUNK), CHUNK)
        reached = lax.broadcasted_iota(jnp.int32, (1, CHUNK), 1) + CHUNK * j < n_c.astype(jnp.int32)
        ms_s[0:1, s] = jnp.where(reached, 256.0 * r[0:1] + r[1:2], -1.0)
        return 0

    lax.fori_loop(0, 8, pack_slots, 0)
    slot_copy = pltpu.make_async_remote_copy(
        src_ref=ms_s, dst_ref=slots_out, send_sem=m_send.at[3], recv_sem=m_recv.at[3], device_id=(x2,), device_id_type=MESH,
    )
    slot_copy.start()

    tot = acc[:, 0:WIDTH]
    num = acc[:, WIDTH : WIDTH + 1]
    c2 = tot / num
    pair_sum = jnp.concatenate([tot[0:1] + tot[1:2], tot[2:3] + tot[3:4]], axis=0)
    pair_num = jnp.concatenate([num[0:1] + num[1:2], num[2:3] + num[3:4]], axis=0)
    c1 = pair_sum / pair_num
    flag[...] = jnp.broadcast_to(acc[0:1, WIDTH + 64 : WIDTH + 65], (8, 128))
    cent[0:2, :] = c1
    cent[2:6, :] = c2
    six = jnp.concatenate([c1, c2, jnp.zeros((2, WIDTH), F32)], axis=0)
    norm = jnp.sum(six * six, axis=1, keepdims=True)
    off_one = 0.5 * (norm[1:2] - norm[0:1])
    off_low = 0.5 * (norm[3:4] - norm[2:3])
    off_high = 0.5 * (norm[5:6] - norm[4:5])
    sixb = jnp.concatenate([six, jnp.zeros((8, WIDTH), F32)], axis=0).astype(BF16)

    def margins(k, _):
        s = pl.ds(pl.multiple_of(k * 512, 512), 512)
        sc = lax.dot_general(sixb, xv[s, :], (((1,), (1,)), ((), ())), preferred_element_type=F32)
        fk = lab_ref[0:1, s]
        mk = lab_ref[1:2, s] != u
        lk = fk != t
        one = (sc[1:2] - sc[0:1] - off_one) / WIDTH
        two = jnp.where(fk == 1, sc[5:6] - sc[4:5] - off_high, sc[3:4] - sc[2:3] - off_low) / WIDTH
        m1[0:1, s] = jnp.where(lk, 0.0, one)
        m2[0:1, s] = jnp.where(lk, 0.0, jnp.where(mk, 0.0, two))
        two_c = jnp.where(mk, 0.0, two)
        vmat[:, s] = stack_rows([*split3(one), *split3(two_c), *split3(two)], 16).astype(BF16)
        return 0

    lax.fori_loop(0, 8, margins, 0)

    def pack_c(j, _):
        r = pack_margins(3, CHUNK * j)
        s = pl.ds(pl.multiple_of(j * CHUNK, CHUNK), CHUNK)
        ms_c[0:1, s] = r[0:1] + r[1:2] + r[2:3]
        ms_c[1:2, s] = r[3:4] + r[4:5] + r[5:6]
        return 0

    def pack_bd(j, _):
        r = pack_margins(1 + j // 2, CHUNK * (j % 2))
        s = pl.ds(pl.multiple_of((j % 2) * CHUNK, CHUNK), CHUNK)
        v = r[6:7] + r[7:8] + r[8:9]

        @pl.when(j < 2)
        def _():
            ms_b[0:1, s] = v

        @pl.when(j >= 2)
        def _():
            ms_d[0:1, s] = v

        return 0

    ms_b[1:2, :] = jnp.broadcast_to(n_b, (1, HALF))
    ms_d[1:2, :] = jnp.zeros((1, HALF), F32)
    lax.fori_loop(0, 4, pack_bd, 0)
    m_copies = [
        pltpu.make_async_remote_copy(
            src_ref=src, dst_ref=dst, send_sem=m_send.at[i], recv_sem=m_recv.at[i], device_id=(d,), device_id_type=MESH,
        )
        for i, (src, dst, d) in enumerate([(ms_b, ml_b, x1), (ms_d, ml_d, x3), (ms_c, ml_c, x2)])
    ]
    m_copies[0].start()
    m_copies[1].start()
    lax.fori_loop(0, 8, pack_c, 0)
    m_copies[2].start()

    def late(j, _):
        compact(0, HEAD + CHUNK * j, HEAD + CHUNK * j)
        return 0

    lax.fori_loop(MID, C_CHUNKS, late, 0)
    late_copy.start()
    last_copy.start()
    spare = pltpu.make_async_copy(ybuf.at[pl.ds(MOST, CAP_ONE - MOST)], rest, load_sem.at[0])
    spare.start()

    def keep(k, _):
        s = pl.ds(pl.multiple_of(k * 256, 256), 256)
        stay = jnp.where(lab_ref[0:1, s] == t, jnp.where(lab_ref[1:2, s] == u, 1.0, 0.0), 0.0)
        eye = lax.broadcasted_iota(jnp.int32, (256, 256), 0) == lax.broadcasted_iota(jnp.int32, (256, 256), 1)
        pick = jnp.where(eye, stay, 0.0).astype(BF16)
        held[s, :] = jnp.dot(pick, xv[s, :], preferred_element_type=F32).astype(BF16)
        return 0

    lax.fori_loop(0, ROWS // 256, keep, 0)

    for c in m_copies[:2]:
        c.wait()
    for j in range(2):
        b_copy(j).wait()
        d_copy(j).wait()
    shift = ml_b[1:2, 0:1].astype(jnp.int32)

    def place(k, _):
        base = k * 256
        s = pl.ds(pl.multiple_of(ROWS + CAP_ONE + base, 256), 256)
        slot = lax.broadcasted_iota(jnp.int32, (256, HALF), 0) + base
        src = lax.broadcasted_iota(jnp.int32, (256, HALF), 1) + shift
        hot = jnp.where(slot == src, 1.0, 0.0).astype(BF16)
        rows = jnp.dot(hot, dland[...], preferred_element_type=F32)

        @pl.when(k < 2)
        def _():
            held[s, :] = (rows + held[s, :].astype(F32)).astype(BF16)

        @pl.when(k >= 2)
        def _():
            held[s, :] = rows.astype(BF16)

        return 0

    lax.fori_loop(0, 4, place, 0)
    dm = stack_rows(list(split3(ml_d[0:1, :])), 16).astype(BF16)
    src = lax.broadcasted_iota(jnp.int32, (HALF, CAP_TWO), 0) + shift
    slot = lax.broadcasted_iota(jnp.int32, (HALF, CAP_TWO), 1)
    moved = jnp.dot(dm, jnp.where(slot == src, 1.0, 0.0).astype(BF16), preferred_element_type=F32)
    moved = moved[0:1] + moved[1:2] + moved[2:3]
    m2[0:1, ROWS + CAP_ONE : ROWS + CAP_ONE + HALF] = moved[:, 0:HALF] + ml_b[0:1, :]
    m2[0:1, ROWS + CAP_ONE + HALF : HELD] = moved[:, HALF:CAP_TWO]
    m_copies[2].wait()
    m1[0:1, ROWS : ROWS + CAP_ONE] = ml_c[0:1, :]
    m2[0:1, ROWS : ROWS + CAP_ONE] = ml_c[1:2, :]

    head_copy.wait()
    for j in range(MID):
        c_copy(j).wait()
    slot_copy.wait()
    slot_store = pltpu.make_async_copy(slots_out, slots_hbm, load_sem.at[1])
    slot_store.start()

    def spread(k, at, size):
        slot = lax.broadcasted_iota(jnp.int32, (CHUNK, size), 0) + k * CHUNK
        hot = jnp.where(slot == slots_out[0:1, at : at + size].astype(jnp.int32), 1.0, 0.0).astype(BF16)
        return jnp.dot(hot, cland[at : at + size, :], preferred_element_type=F32)

    def spread_first(k, _):
        s = pl.ds(pl.multiple_of(ROWS + k * CHUNK, CHUNK), CHUNK)
        held[s, :] = spread(k, 0, LATE).astype(BF16)
        return 0

    lax.fori_loop(0, CAP_ONE // CHUNK, spread_first, 0)

    def spread_more(at, size):
        def body(k, _):
            s = pl.ds(pl.multiple_of(ROWS + k * CHUNK, CHUNK), CHUNK)
            held[s, :] = (held[s, :].astype(F32) + spread(k, at, size)).astype(BF16)
            return 0

        lax.fori_loop(at // CHUNK, CAP_ONE // CHUNK, body, 0)

    spare.wait()
    slot_store.wait()
    late_copy.wait()
    spread_more(LATE, SPLIT - LATE)
    last_copy.wait()
    spread_more(SPLIT, MOST - SPLIT)


def rest_kernel(rest, extra, send_sem, recv_sem):
    me = lax.axis_index("cube")
    other = me + 64 - 128 * (me // 64)
    barrier = pltpu.get_barrier_semaphore()
    pl.semaphore_signal(barrier, inc=1, device_id=(other,), device_id_type=MESH)
    pl.semaphore_wait(barrier, 1)
    copy = pltpu.make_async_remote_copy(
        src_ref=rest, dst_ref=extra, send_sem=send_sem, recv_sem=recv_sem, device_id=(other,), device_id_type=MESH
    )
    copy.start()
    copy.wait()


PIECES = 14
END = ROWS + CAP_ONE - CHUNK


def store_kernel(held, m1, m2, cent, held_out, m1_out, m2_out, cent_out, sem):
    step = HELD // PIECES
    copies = [
        pltpu.make_async_copy(held.at[pl.ds(i * step, step)], held_out.at[pl.ds(i * step, step)], sem.at[i])
        for i in range(PIECES)
    ]
    for i, (src, dst) in enumerate([(m1, m1_out), (m2, m2_out), (cent, cent_out)]):
        copies.append(pltpu.make_async_copy(src, dst, sem.at[PIECES + i]))
    for c in copies:
        c.start()
    for c in copies:
        c.wait()


def add_kernel(held, slots, extra, held_out, rows, sem):
    load = pltpu.make_async_copy(held.at[pl.ds(END, CHUNK)], rows, sem)
    load.start()
    load.wait()
    slot = lax.broadcasted_iota(jnp.int32, (CHUNK, CAP_ONE - MOST), 0) + CAP_ONE - CHUNK
    hot = jnp.where(slot == slots[0:1, MOST:CAP_ONE].astype(jnp.int32), 1.0, 0.0).astype(BF16)
    more = jnp.dot(hot, extra[...], preferred_element_type=F32)
    rows[...] = (rows[...].astype(F32) + more).astype(BF16)
    back = pltpu.make_async_copy(rows, held_out.at[pl.ds(END, CHUNK)], sem)
    back.start()
    back.wait()


def local(vectors, child_labels):
    in_vmem = pl.BlockSpec(memory_space=pltpu.VMEM)
    anywhere = pl.BlockSpec(memory_space=pl.ANY)
    shapes = [((HELD, WIDTH), BF16), ((1, ROWS + CAP_ONE), F32), ((1, HELD), F32), ((6, WIDTH), F32)]
    dma = pltpu.SemaphoreType.DMA
    held_shape = jax.ShapeDtypeStruct((HELD, WIDTH), BF16)
    rest_shape = jax.ShapeDtypeStruct((CAP_ONE - MOST, WIDTH), BF16)
    *parts, flag, rest, slots = pl.pallas_call(
        exchange_kernel,
        out_shape=(
            *(pltpu.VMEM(s, d) for s, d in shapes + [((8, 128), F32)]),
            rest_shape,
            jax.ShapeDtypeStruct((1, CAP_ONE), F32),
        ),
        in_specs=[anywhere, anywhere],
        out_specs=(in_vmem,) * 5 + (anywhere,) * 2,
        scratch_shapes=[
            pltpu.VMEM((ROWS, WIDTH), BF16),
            pltpu.VMEM((2, ROWS), jnp.int32),
            pltpu.VMEM((PACKED, WIDTH), BF16),
            pltpu.VMEM((MOST, WIDTH), BF16),
            pltpu.VMEM((HALF, WIDTH), BF16),
            pltpu.VMEM((CHUNK, ROWS), BF16),
            pltpu.VMEM((8, ROWS), jnp.int32),
            pltpu.VMEM((4, WIDTH + 128), F32),
            pltpu.VMEM((6, 4, WIDTH + 128), F32),
            pltpu.VMEM((8, 4, WIDTH + 128), F32),
            pltpu.VMEM((16, ROWS), BF16),
            pltpu.VMEM((2, CAP_ONE), F32),
            pltpu.VMEM((2, HALF), F32),
            pltpu.VMEM((2, HALF), F32),
            pltpu.VMEM((1, CAP_ONE), F32),
            pltpu.VMEM((1, CAP_ONE), F32),
            pltpu.VMEM((2, CAP_ONE), F32),
            pltpu.VMEM((2, HALF), F32),
            pltpu.VMEM((2, HALF), F32),
            dma((ROWS // LOAD + 1,)),
            dma((8,)),
            dma((8,)),
            dma((C_CHUNKS + 5,)),
            dma((C_CHUNKS + 5,)),
            dma((4,)),
            dma((4,)),
        ],
        compiler_params=pltpu.CompilerParams(
            collective_id=0, has_side_effects=True, vmem_limit_bytes=44 << 20
        ),
        name="exchange",
    )(vectors, child_labels)
    send_rest = pl.pallas_call(
        rest_kernel,
        out_shape=rest_shape,
        in_specs=[anywhere],
        out_specs=anywhere,
        scratch_shapes=[dma, dma],
        compiler_params=pltpu.CompilerParams(collective_id=1, has_side_effects=True),
        name="rest",
    )
    held, m1, m2, cent = pl.pallas_call(
        store_kernel,
        out_shape=tuple(jax.ShapeDtypeStruct(s, d) for s, d in shapes),
        in_specs=[in_vmem] * 4,
        out_specs=(anywhere,) * 4,
        scratch_shapes=[dma((PIECES + 3,))],
        compiler_params=pltpu.CompilerParams(vmem_limit_bytes=16 << 20),
        name="store",
    )(*parts)
    add_rest = pl.pallas_call(
        add_kernel,
        out_shape=held_shape,
        in_specs=[anywhere, in_vmem, in_vmem],
        out_specs=anywhere,
        scratch_shapes=[pltpu.VMEM((CHUNK, WIDTH), BF16), dma],
        input_output_aliases={0: 0},
        compiler_params=pltpu.CompilerParams(vmem_limit_bytes=16 << 20),
        name="add",
    )

    steps = (flag[0, 0] > MOST).astype(jnp.int32)

    def step(carry):
        done, rows = carry
        return done + 1, add_rest(rows, slots, send_rest(rest))

    _, held = lax.while_loop(lambda carry: carry[0] < steps, step, (jnp.int32(0), held))
    return held, m1.reshape(-1), m2.reshape(-1), cent


def solution(mesh):
    return jax.shard_map(
        local,
        mesh=mesh,
        in_specs=(P("cube", None), P(None, "cube")),
        out_specs=(P("cube", None), P("cube"), P("cube"), P()),
        check_vma=False,
    )
```

```python
import jax
import jax.numpy as jnp
from jax import lax
from jax.experimental import pallas as pl
from jax.experimental.pallas import tpu as pltpu
from jax.sharding import PartitionSpec as P

MESH = pl.DeviceIdType.MESH
ROWS = 4096
WIDTH = 768
CAP_ONE = 2048
CAP_TWO = 1024
HALF = 512
LOAD = 1024
AHEAD = 4
PIECE = 512
CHUNK = 256
HELD = ROWS + CAP_ONE + CAP_TWO
F32 = jnp.float32
BF16 = jnp.bfloat16

MOST = 1792
SPLIT = 1536
HEAD = 128
MID = 4
C_CHUNKS = 8
B_AT = HEAD + C_CHUNKS * CHUNK
D_AT = B_AT + HALF
PACKED = D_AT + HALF
SUM_ROWS = 16
LATE = HEAD + MID * CHUNK


def split3(v):
    hi = v.astype(BF16).astype(F32)
    mid = (v - hi).astype(BF16).astype(F32)
    lo = v - hi - mid
    return hi, mid, lo


def stack_rows(rows, count):
    at = lax.broadcasted_iota(jnp.int32, (count, rows[0].shape[1]), 0)
    out = jnp.zeros(at.shape, rows[0].dtype)
    for k, row in enumerate(rows):
        out = jnp.where(at == k, row, out)
    return out


def exchange_kernel(
    x_ref, lab_any,
    held, m1, m2, cent, flag, rest, slots_hbm,
    xv, lab_ref, ybuf, cland, dland, lhs, rk, acc, accs, arl, vmat, ms_c, ms_b, ms_d, ms_s, slots_out, ml_c, ml_b, ml_d,
    load_sem, ar_send, ar_recv, row_send, row_recv, m_send, m_recv,
):
    me = lax.axis_index("cube")
    loads = [
        pltpu.make_async_copy(x_ref.at[pl.ds(i * LOAD, LOAD)], xv.at[pl.ds(i * LOAD, LOAD)], load_sem.at[i])
        for i in range(ROWS // LOAD)
    ]
    lab_load = pltpu.make_async_copy(lab_any, lab_ref, load_sem.at[ROWS // LOAD])
    lab_load.start()
    for c in loads[:AHEAD]:
        c.start()
    xi = me // 32
    yi = (me // 8) % 4
    zi = (me // 2) % 4
    t = me // 64
    u = xi % 2

    def three(i, stride):
        return [
            me + stride * (1 - 2 * (i % 2)),
            me + stride * (2 - 4 * (i // 2)),
            me + stride * (3 - 2 * i),
        ]

    x1, x2, x3 = three(xi, 32)
    z1, z2, _ = three(zi, 2)
    y1, y2, _ = three(yi, 8)
    phases = [[x1, x2, x3], [z1], [z2], [y1], [y2], [me + 1 - 2 * (me % 2)]]
    slots = [0, 3, 4, 5, 6, 7]
    partners = [d for phase in phases for d in phase]

    barrier = pltpu.get_barrier_semaphore()
    for d in partners:
        pl.semaphore_signal(barrier, inc=1, device_id=(d,), device_id_type=MESH)

    lab_load.wait()

    first = lab_ref[0:1, :]
    later = lab_ref[1:2, :]
    leave = first != t
    move = later != u
    f_leave = jnp.where(leave, 1.0, 0.0)
    f_move = jnp.where(move, 1.0, 0.0)
    f_b = f_move * (1.0 - f_leave)
    f_d = f_move * f_leave
    f_c = f_leave * (1.0 - f_move)
    kinds = stack_rows([f_leave, f_b, f_d, f_c], 16)
    tri = jnp.where(
        lax.broadcasted_iota(jnp.int32, (256, 256), 0) <= lax.broadcasted_iota(jnp.int32, (256, 256), 1), 1.0, 0.0
    ).astype(BF16)
    carry = jnp.full((16, 1), -1.0, F32)
    for k in range(ROWS // 256):
        part = kinds[:, 256 * k : 256 * k + 256]
        run = jnp.dot(part.astype(BF16), tri, preferred_element_type=F32) + carry
        carry = carry + jnp.sum(part, axis=1, keepdims=True)
        place = run.astype(jnp.int32)
        s = pl.ds(256 * k, 256)
        lv = leave[:, 256 * k : 256 * k + 256]
        mv = move[:, 256 * k : 256 * k + 256]
        none = jnp.full((1, 256), -1, jnp.int32)
        rk[0:1, s] = jnp.where(mv, none, jnp.where(lv, place[3:4], none))
        rk[1:2, s] = jnp.where(lv, none, jnp.where(mv, place[1:2], none))
        rk[2:3, s] = jnp.where(lv, jnp.where(mv, place[2:3], none), none)
        rk[3:4, s] = jnp.where(lv, place[0:1], none)
    n_b = carry[1:2, 0:1] + 1.0
    n_c = carry[3:4, 0:1] + 1.0

    def one_hot(row, base):
        for k in range(ROWS // 256):
            s = pl.ds(256 * k, 256)
            at = lax.broadcasted_iota(jnp.int32, (CHUNK, 256), 0)
            want = rk[pl.ds(row, 1), s] - base
            lhs[0:CHUNK, s] = jnp.where(at == want, 1.0, 0.0).astype(BF16)

    def hot_piece(row, base, count, at, size):
        slot = lax.broadcasted_iota(jnp.int32, (count, size), 0)
        return jnp.where(slot == rk[pl.ds(row, 1), pl.ds(at, size)] - base, 1.0, 0.0).astype(BF16)

    out = jnp.zeros((HEAD, WIDTH), F32)
    for i, c in enumerate(loads):
        c.wait()
        if i + AHEAD < len(loads):
            loads[i + AHEAD].start()
        hot = hot_piece(0, 0, HEAD, i * LOAD, LOAD)
        out = out + jnp.dot(hot, xv[pl.ds(i * LOAD, LOAD), :], preferred_element_type=F32)
    ybuf[0:HEAD, :] = out.astype(BF16)
    pl.semaphore_wait(barrier, len(partners))

    LAST = len(phases) - 1

    def ar_copies(p):
        base = slots[p]
        return [
            pltpu.make_async_remote_copy(
                src_ref=accs.at[p], dst_ref=arl.at[base + i], send_sem=ar_send.at[base + i],
                recv_sem=ar_recv.at[base + i], device_id=(d,), device_id_type=MESH,
            )
            for i, d in enumerate(phases[p])
        ]

    def ar_start(p):
        for c in ar_copies(p):
            c.start()

    def ar_finish(p):
        for c in ar_copies(p):
            c.wait()
        base = slots[p]
        total = accs[p] + arl[base]
        most = jnp.maximum(accs[p], arl[base])
        if len(phases[p]) == 3:
            total = total + (arl[base + 1] + arl[base + 2])
            most = jnp.maximum(most, jnp.maximum(arl[base + 1], arl[base + 2]))
        is_max = lax.broadcasted_iota(jnp.int32, total.shape, 1) >= WIDTH + 64
        total = jnp.where(is_max, most, total)
        if p < LAST:
            accs[p + 1] = total
        else:
            acc[...] = total

    def rows_copy(k, src, dst, start, count, to):
        return pltpu.make_async_remote_copy(
            src_ref=ybuf.at[pl.ds(pl.multiple_of(src, HEAD), count)],
            dst_ref=dst.at[pl.ds(pl.multiple_of(start, HEAD), count)],
            send_sem=row_send.at[k], recv_sem=row_recv.at[k], device_id=(to,), device_id_type=MESH,
        )

    def c_copy(j, count=CHUNK):
        src = HEAD + j * CHUNK
        return rows_copy(4 + j, src, cland, src, count, x2)

    def b_copy(j):
        return rows_copy(2 * j, B_AT + j * CHUNK, held, ROWS + CAP_ONE + j * CHUNK, CHUNK, x1)

    def d_copy(j):
        return rows_copy(2 * j + 1, D_AT + j * CHUNK, dland, j * CHUNK, CHUNK, x3)

    head_copy = rows_copy(4 + C_CHUNKS, 0, cland, 0, HEAD, x2)
    late_copy = c_copy(MID, SPLIT - LATE)
    last_copy = rows_copy(4 + MID + 1, SPLIT, cland, SPLIT, MOST - SPLIT, x2)
    head_copy.start()

    def compact(row, base, to):
        res = jnp.zeros((CHUNK, WIDTH), F32)
        for k in range(ROWS // PIECE):
            hot = hot_piece(row, base, CHUNK, k * PIECE, PIECE)
            res = res + jnp.dot(hot, xv[pl.ds(k * PIECE, PIECE), :], preferred_element_type=F32)
        ybuf[pl.ds(pl.multiple_of(to, HEAD), CHUNK), :] = res.astype(BF16)

    group = 2 * first + later
    masks = stack_rows([jnp.where(group == g, 1.0, 0.0) for g in range(4)], SUM_ROWS)
    count = jnp.sum(masks[0:4], axis=1, keepdims=True)
    res = jnp.zeros((CHUNK + SUM_ROWS, WIDTH), F32)
    for k in range(ROWS // PIECE):
        hot = hot_piece(0, HEAD, CHUNK, k * PIECE, PIECE)
        both = jnp.concatenate([hot, masks[:, k * PIECE : (k + 1) * PIECE].astype(BF16)], axis=0)
        res = res + jnp.dot(both, xv[pl.ds(k * PIECE, PIECE), :], preferred_element_type=F32)
    ybuf[HEAD : HEAD + CHUNK, :] = res[0:CHUNK].astype(BF16)
    accs[0, :, 0:WIDTH] = res[CHUNK : CHUNK + 4]
    is_max = lax.broadcasted_iota(jnp.int32, (4, WIDTH + 128), 1) >= WIDTH + 64
    accs[0, :, WIDTH:] = jnp.where(is_max[:, WIDTH:], n_c, count)
    ar_start(0)
    c_copy(0).start()

    def ar_step(p):
        ar_finish(p)
        if p < LAST:
            ar_start(p + 1)

    def early_bd(k, _):
        j = k // 2
        compact(1 + k % 2, CHUNK * j, B_AT + HALF * (k % 2) + CHUNK * j)

        @pl.when(k % 2 == 1)
        def _():
            b_copy(j).start()
            d_copy(j).start()

        for p in range(4):
            @pl.when(k == p)
            def _(p=p):
                ar_step(p)

        return 0

    lax.fori_loop(0, 4, early_bd, 0)

    def early_c(j, _):
        compact(0, HEAD + CHUNK * j, HEAD + CHUNK * j)
        c_copy(j).start()

        for p in range(4, len(phases)):
            @pl.when(j == p - 3)
            def _(p=p):
                ar_step(p)

        return 0

    lax.fori_loop(1, MID, early_c, 0)

    def pack_margins(row, base):
        one_hot(row, base)
        return lax.dot_general(
            vmat[...], lhs[0:CHUNK, :], (((1,), (1,)), ((), ())), preferred_element_type=F32
        )

    slot = rk[3:4, :]
    high = slot // 256
    vmat[...] = stack_rows([high.astype(F32), (slot - 256 * high).astype(F32)], 16).astype(BF16)

    def pack_slots(j, _):
        r = pack_margins(0, CHUNK * j)
        s = pl.ds(pl.multiple_of(j * CHUNK, CHUNK), CHUNK)
        reached = lax.broadcasted_iota(jnp.int32, (1, CHUNK), 1) + CHUNK * j < n_c.astype(jnp.int32)
        ms_s[0:1, s] = jnp.where(reached, 256.0 * r[0:1] + r[1:2], -1.0)
        return 0

    lax.fori_loop(0, 8, pack_slots, 0)
    slot_copy = pltpu.make_async_remote_copy(
        src_ref=ms_s, dst_ref=slots_out, send_sem=m_send.at[3], recv_sem=m_recv.at[3], device_id=(x2,), device_id_type=MESH,
    )
    slot_copy.start()

    tot = acc[:, 0:WIDTH]
    num = acc[:, WIDTH : WIDTH + 1]
    c2 = tot / num
    pair_sum = jnp.concatenate([tot[0:1] + tot[1:2], tot[2:3] + tot[3:4]], axis=0)
    pair_num = jnp.concatenate([num[0:1] + num[1:2], num[2:3] + num[3:4]], axis=0)
    c1 = pair_sum / pair_num
    flag[...] = jnp.where(acc[0:1, WIDTH + 64 : WIDTH + 65] > MOST, 1, 0)
    cent[0:2, :] = c1
    cent[2:6, :] = c2
    six = jnp.concatenate([c1, c2, jnp.zeros((2, WIDTH), F32)], axis=0)
    norm = jnp.sum(six * six, axis=1, keepdims=True)
    off_one = 0.5 * (norm[1:2] - norm[0:1])
    off_low = 0.5 * (norm[3:4] - norm[2:3])
    off_high = 0.5 * (norm[5:6] - norm[4:5])
    sixb = jnp.concatenate([six, jnp.zeros((8, WIDTH), F32)], axis=0).astype(BF16)

    def margins(k, _):
        s = pl.ds(pl.multiple_of(k * 512, 512), 512)
        sc = lax.dot_general(sixb, xv[s, :], (((1,), (1,)), ((), ())), preferred_element_type=F32)
        fk = lab_ref[0:1, s]
        mk = lab_ref[1:2, s] != u
        lk = fk != t
        one = (sc[1:2] - sc[0:1] - off_one) / WIDTH
        two = jnp.where(fk == 1, sc[5:6] - sc[4:5] - off_high, sc[3:4] - sc[2:3] - off_low) / WIDTH
        m1[0:1, s] = jnp.where(lk, 0.0, one)
        m2[0:1, s] = jnp.where(lk, 0.0, jnp.where(mk, 0.0, two))
        two_c = jnp.where(mk, 0.0, two)
        vmat[:, s] = stack_rows([*split3(one), *split3(two_c), *split3(two)], 16).astype(BF16)
        return 0

    lax.fori_loop(0, 8, margins, 0)

    def pack_c(j, _):
        r = pack_margins(3, CHUNK * j)
        s = pl.ds(pl.multiple_of(j * CHUNK, CHUNK), CHUNK)
        ms_c[0:1, s] = r[0:1] + r[1:2] + r[2:3]
        ms_c[1:2, s] = r[3:4] + r[4:5] + r[5:6]
        return 0

    def pack_bd(j, _):
        r = pack_margins(1 + j // 2, CHUNK * (j % 2))
        s = pl.ds(pl.multiple_of((j % 2) * CHUNK, CHUNK), CHUNK)
        v = r[6:7] + r[7:8] + r[8:9]

        @pl.when(j < 2)
        def _():
            ms_b[0:1, s] = v

        @pl.when(j >= 2)
        def _():
            ms_d[0:1, s] = v

        return 0

    ms_b[1:2, :] = jnp.broadcast_to(n_b, (1, HALF))
    ms_d[1:2, :] = jnp.zeros((1, HALF), F32)
    lax.fori_loop(0, 4, pack_bd, 0)
    m_copies = [
        pltpu.make_async_remote_copy(
            src_ref=src, dst_ref=dst, send_sem=m_send.at[i], recv_sem=m_recv.at[i], device_id=(d,), device_id_type=MESH,
        )
        for i, (src, dst, d) in enumerate([(ms_b, ml_b, x1), (ms_d, ml_d, x3), (ms_c, ml_c, x2)])
    ]
    m_copies[0].start()
    m_copies[1].start()
    lax.fori_loop(0, 8, pack_c, 0)
    m_copies[2].start()

    def late(j, _):
        compact(0, HEAD + CHUNK * j, HEAD + CHUNK * j)
        return 0

    lax.fori_loop(MID, C_CHUNKS, late, 0)
    late_copy.start()
    last_copy.start()
    spare = pltpu.make_async_copy(ybuf.at[pl.ds(MOST, CAP_ONE - MOST)], rest, load_sem.at[0])
    spare.start()

    def keep(k, _):
        s = pl.ds(pl.multiple_of(k * 256, 256), 256)
        stay = jnp.where(lab_ref[0:1, s] == t, jnp.where(lab_ref[1:2, s] == u, 1.0, 0.0), 0.0)
        eye = lax.broadcasted_iota(jnp.int32, (256, 256), 0) == lax.broadcasted_iota(jnp.int32, (256, 256), 1)
        pick = jnp.where(eye, stay, 0.0).astype(BF16)
        held[s, :] = jnp.dot(pick, xv[s, :], preferred_element_type=F32).astype(BF16)
        return 0

    lax.fori_loop(0, ROWS // 256, keep, 0)

    for c in m_copies[:2]:
        c.wait()
    for j in range(2):
        b_copy(j).wait()
        d_copy(j).wait()
    shift = ml_b[1:2, 0:1].astype(jnp.int32)

    def place(k, _):
        base = k * 256
        s = pl.ds(pl.multiple_of(ROWS + CAP_ONE + base, 256), 256)
        slot = lax.broadcasted_iota(jnp.int32, (256, HALF), 0) + base
        src = lax.broadcasted_iota(jnp.int32, (256, HALF), 1) + shift
        hot = jnp.where(slot == src, 1.0, 0.0).astype(BF16)
        rows = jnp.dot(hot, dland[...], preferred_element_type=F32)

        @pl.when(k < 2)
        def _():
            held[s, :] = (rows + held[s, :].astype(F32)).astype(BF16)

        @pl.when(k >= 2)
        def _():
            held[s, :] = rows.astype(BF16)

        return 0

    lax.fori_loop(0, 4, place, 0)
    dm = stack_rows(list(split3(ml_d[0:1, :])), 16).astype(BF16)
    src = lax.broadcasted_iota(jnp.int32, (HALF, CAP_TWO), 0) + shift
    slot = lax.broadcasted_iota(jnp.int32, (HALF, CAP_TWO), 1)
    moved = jnp.dot(dm, jnp.where(slot == src, 1.0, 0.0).astype(BF16), preferred_element_type=F32)
    moved = moved[0:1] + moved[1:2] + moved[2:3]
    m2[0:1, ROWS + CAP_ONE : ROWS + CAP_ONE + HALF] = moved[:, 0:HALF] + ml_b[0:1, :]
    m2[0:1, ROWS + CAP_ONE + HALF : HELD] = moved[:, HALF:CAP_TWO]
    m_copies[2].wait()
    m1[0:1, ROWS : ROWS + CAP_ONE] = ml_c[0:1, :]
    m2[0:1, ROWS : ROWS + CAP_ONE] = ml_c[1:2, :]

    head_copy.wait()
    for j in range(MID):
        c_copy(j).wait()
    slot_copy.wait()
    slot_store = pltpu.make_async_copy(slots_out, slots_hbm, load_sem.at[1])
    slot_store.start()

    def spread(k, at, size):
        slot = lax.broadcasted_iota(jnp.int32, (CHUNK, size), 0) + k * CHUNK
        hot = jnp.where(slot == slots_out[0:1, at : at + size].astype(jnp.int32), 1.0, 0.0).astype(BF16)
        return jnp.dot(hot, cland[at : at + size, :], preferred_element_type=F32)

    def spread_first(k, _):
        s = pl.ds(pl.multiple_of(ROWS + k * CHUNK, CHUNK), CHUNK)
        held[s, :] = spread(k, 0, LATE).astype(BF16)
        return 0

    lax.fori_loop(0, CAP_ONE // CHUNK, spread_first, 0)

    def spread_more(at, size):
        def body(k, _):
            s = pl.ds(pl.multiple_of(ROWS + k * CHUNK, CHUNK), CHUNK)
            held[s, :] = (held[s, :].astype(F32) + spread(k, at, size)).astype(BF16)
            return 0

        lax.fori_loop(at // CHUNK, CAP_ONE // CHUNK, body, 0)

    spare.wait()
    slot_store.wait()
    late_copy.wait()
    spread_more(LATE, SPLIT - LATE)
    last_copy.wait()
    spread_more(SPLIT, MOST - SPLIT)


def rest_kernel(rest, extra, send_sem, recv_sem):
    me = lax.axis_index("cube")
    other = me + 64 - 128 * (me // 64)
    barrier = pltpu.get_barrier_semaphore()
    pl.semaphore_signal(barrier, inc=1, device_id=(other,), device_id_type=MESH)
    pl.semaphore_wait(barrier, 1)
    copy = pltpu.make_async_remote_copy(
        src_ref=rest, dst_ref=extra, send_sem=send_sem, recv_sem=recv_sem, device_id=(other,), device_id_type=MESH
    )
    copy.start()
    copy.wait()


PIECES = 14
END = ROWS + CAP_ONE - CHUNK


def store_kernel(held, m1, m2, cent, held_out, m1_out, m2_out, cent_out, sem):
    step = HELD // PIECES
    copies = [
        pltpu.make_async_copy(held.at[pl.ds(i * step, step)], held_out.at[pl.ds(i * step, step)], sem.at[i])
        for i in range(PIECES)
    ]
    for i, (src, dst) in enumerate([(m1, m1_out), (m2, m2_out), (cent, cent_out)]):
        copies.append(pltpu.make_async_copy(src, dst, sem.at[PIECES + i]))
    for c in copies:
        c.start()
    for c in copies:
        c.wait()


def add_kernel(held, slots, extra, held_out, rows, sem):
    load = pltpu.make_async_copy(held.at[pl.ds(END, CHUNK)], rows, sem)
    load.start()
    load.wait()
    slot = lax.broadcasted_iota(jnp.int32, (CHUNK, CAP_ONE - MOST), 0) + CAP_ONE - CHUNK
    hot = jnp.where(slot == slots[0:1, MOST:CAP_ONE].astype(jnp.int32), 1.0, 0.0).astype(BF16)
    more = jnp.dot(hot, extra[...], preferred_element_type=F32)
    rows[...] = (rows[...].astype(F32) + more).astype(BF16)
    back = pltpu.make_async_copy(rows, held_out.at[pl.ds(END, CHUNK)], sem)
    back.start()
    back.wait()


def local(vectors, child_labels):
    in_vmem = pl.BlockSpec(memory_space=pltpu.VMEM)
    anywhere = pl.BlockSpec(memory_space=pl.ANY)
    shapes = [((HELD, WIDTH), BF16), ((1, ROWS + CAP_ONE), F32), ((1, HELD), F32), ((6, WIDTH), F32)]
    dma = pltpu.SemaphoreType.DMA
    held_shape = jax.ShapeDtypeStruct((HELD, WIDTH), BF16)
    rest_shape = jax.ShapeDtypeStruct((CAP_ONE - MOST, WIDTH), BF16)
    *parts, flag, rest, slots = pl.pallas_call(
        exchange_kernel,
        out_shape=(
            *(pltpu.VMEM(s, d) for s, d in shapes + [((1, 1), jnp.int32)]),
            rest_shape,
            jax.ShapeDtypeStruct((1, CAP_ONE), F32),
        ),
        in_specs=[anywhere, anywhere],
        out_specs=(in_vmem,) * 5 + (anywhere,) * 2,
        scratch_shapes=[
            pltpu.VMEM((ROWS, WIDTH), BF16),
            pltpu.VMEM((2, ROWS), jnp.int32),
            pltpu.VMEM((PACKED, WIDTH), BF16),
            pltpu.VMEM((MOST, WIDTH), BF16),
            pltpu.VMEM((HALF, WIDTH), BF16),
            pltpu.VMEM((CHUNK, ROWS), BF16),
            pltpu.VMEM((8, ROWS), jnp.int32),
            pltpu.VMEM((4, WIDTH + 128), F32),
            pltpu.VMEM((6, 4, WIDTH + 128), F32),
            pltpu.VMEM((8, 4, WIDTH + 128), F32),
            pltpu.VMEM((16, ROWS), BF16),
            pltpu.VMEM((2, CAP_ONE), F32),
            pltpu.VMEM((2, HALF), F32),
            pltpu.VMEM((2, HALF), F32),
            pltpu.VMEM((1, CAP_ONE), F32),
            pltpu.VMEM((1, CAP_ONE), F32),
            pltpu.VMEM((2, CAP_ONE), F32),
            pltpu.VMEM((2, HALF), F32),
            pltpu.VMEM((2, HALF), F32),
            dma((ROWS // LOAD + 1,)),
            dma((8,)),
            dma((8,)),
            dma((C_CHUNKS + 5,)),
            dma((C_CHUNKS + 5,)),
            dma((4,)),
            dma((4,)),
        ],
        compiler_params=pltpu.CompilerParams(
            collective_id=0, has_side_effects=True, vmem_limit_bytes=44 << 20
        ),
        name="exchange",
    )(vectors, child_labels)
    send_rest = pl.pallas_call(
        rest_kernel,
        out_shape=rest_shape,
        in_specs=[anywhere],
        out_specs=anywhere,
        scratch_shapes=[dma, dma],
        compiler_params=pltpu.CompilerParams(collective_id=1, has_side_effects=True),
        name="rest",
    )
    held, m1, m2, cent = pl.pallas_call(
        store_kernel,
        out_shape=tuple(jax.ShapeDtypeStruct(s, d) for s, d in shapes),
        in_specs=[in_vmem] * 4,
        out_specs=(anywhere,) * 4,
        scratch_shapes=[dma((PIECES + 3,))],
        compiler_params=pltpu.CompilerParams(vmem_limit_bytes=16 << 20),
        name="store",
    )(*parts)
    add_rest = pl.pallas_call(
        add_kernel,
        out_shape=held_shape,
        in_specs=[anywhere, in_vmem, in_vmem],
        out_specs=anywhere,
        scratch_shapes=[pltpu.VMEM((CHUNK, WIDTH), BF16), dma],
        input_output_aliases={0: 0},
        compiler_params=pltpu.CompilerParams(vmem_limit_bytes=16 << 20),
        name="add",
    )

    steps = flag.reshape(())

    def step(carry):
        done, rows = carry
        return done + 1, add_rest(rows, slots, send_rest(rest))

    _, held = lax.while_loop(lambda carry: carry[0] < steps, step, (jnp.int32(0), held))
    return held, m1.reshape(-1), m2.reshape(-1), cent


def solution(mesh):
    return jax.shard_map(
        local,
        mesh=mesh,
        in_specs=(P("cube", None), P(None, "cube")),
        out_specs=(P("cube", None), P("cube"), P("cube"), P()),
        check_vma=False,
    )
```
